32 devices in a mesh: req: 16 (over z, y, core), tok: 2 (over x).
Axes of the slice: x: 2, y: 2, z: 4, core: 2. Of those that a mesh axis runs over, the one named last changes fastest.
Arguments:
- hidden_in: bfloat16 [32, 256, 2560], P('req', 'tok'), may hold values from -40 to 40
- cache_keys: bfloat16 [32, 4096, 320], P('req', None, 'tok'), may hold values from -100 to 100
- stored_cache_values: bfloat16 [32, 4096, 320], P('req', None, 'tok'), may hold values from -5 to 5
- cache_lengths: int32 [32], P('req'), may hold values from 0 to 16384, as said below
- live_slots: int32 [32], replicated, may hold values from 0 to 1, as said below
- attn_gain: float32 [2560], replicated, may hold values from 0.1 to 1.9
- w_query: bfloat16 [2560, 1280], P(None, 'tok'), may hold values from -0.125 to 0.125
- key_weight: bfloat16 [2560, 320], P(None, 'tok'), may hold values from -0.125 to 0.125
- value_weight: bfloat16 [2560, 320], P(None, 'tok'), may hold values from -0.125 to 0.125
- w_out: bfloat16 [1280, 2560], P('tok'), may hold values from -0.15625 to 0.15625
- mlp_gain: float32 [2560], replicated, may hold values from 0.1 to 1.9
- w_gate: bfloat16 [2560, 3584], P(None, 'tok'), may hold values from -0.125 to 0.125
- w_up: bfloat16 [2560, 3584], P(None, 'tok'), may hold values from -0.125 to 0.125
- w_down: bfloat16 [3584, 2560], P('tok'), may hold values from -0.09375 to 0.09375
Outputs:
- hidden_out: bfloat16 [32, 256, 2560], P('req', 'tok')
- new_keys: bfloat16 [32, 256, 320], P('req', None, 'tok')
- new_values: bfloat16 [32, 256, 320], P('req', None, 'tok')
The draws below stay inside these ranges and needn't reach their ends.
Inputs may be any that keep to these rules, and one draw needn't show every extreme that they name: `live_slots`: exactly 16 of the 32 slots are live; the 2 slots of one index of req hold 0, 1 or 2 live requests, and some index holds two. `cache_lengths`: 0 for a slot that is not live; some live slot has exactly 16384.
All inputs are finite; a program needn't handle non-finite values.
Results may differ from the reference program's by a relative error of at most 0.0095.
Values may be sent and summed in bfloat16 or wider, within the bound.
A program may use at most 192 MiB of HBM per device.

```python
import jax
import jax.numpy as jnp
from jax import lax

MODEL_DIM = 2560
QUERY_HEADS = 16
KEY_VALUE_HEADS = 4
HEAD_DIM = 80
FFW = 3584
NEW_TOKENS = 256
WINDOW_POSITIONS = 4096
LMAX = 16384
ALL_REQUEST_SLOTS = 32
REQUESTS = 16


def plan_slots(key):
    base_key = jax.random.fold_in(key, 17)
    order_key, pick_key, length_key = jax.random.split(base_key, 3)
    order = jax.random.permutation(order_key, REQUESTS)
    ranks = jnp.zeros((REQUESTS,), jnp.int32).at[order].set(jnp.arange(REQUESTS, dtype=jnp.int32))
    quota = max(1, REQUESTS // 8)
    counts = jnp.where(ranks < quota, 2, jnp.where(ranks < 2 * quota, 0, 1))
    picks = jax.random.randint(pick_key, (REQUESTS,), 0, 2)
    first_slot = (counts == 2) | (counts == 1) & (picks == 0)
    second_slot = (counts == 2) | (counts == 1) & (picks == 1)
    alive = jnp.stack([first_slot, second_slot], axis=1).reshape(ALL_REQUEST_SLOTS).astype(jnp.int32)
    factors = jax.random.randint(length_key, (3, ALL_REQUEST_SLOTS), 0, LMAX + 1)
    lengths = factors[0] * factors[1] // LMAX * factors[2] // LMAX
    longest = jnp.repeat(ranks == 0, 2) & (jnp.arange(ALL_REQUEST_SLOTS) % 2 == 0)
    lengths = jnp.where(longest, LMAX, lengths)
    return (alive, (lengths * alive).astype(jnp.int32))


def draw_live_slots(key, part):
    return plan_slots(key)[0]


def draw_cache_lengths(key, part):
    return plan_slots(key)[1]


def draw_hidden_in(key, part):
    row_key, column_key, base_key = jax.random.split(jax.random.fold_in(key, 29), 3)
    target_shape = (ALL_REQUEST_SLOTS, NEW_TOKENS, MODEL_DIM)
    row_scale = jnp.exp(jax.random.uniform(row_key, (ALL_REQUEST_SLOTS, NEW_TOKENS, 1), jnp.float32, -1.15, 1.15))
    column_scale = jnp.exp(jax.random.uniform(column_key, (1, 1, MODEL_DIM), jnp.float32, -1.15, 1.15))
    starting_offset = jnp.clip(jax.random.normal(base_key, target_shape, jnp.float32), -4.0, 4.0)
    return (starting_offset * row_scale * column_scale).astype(jnp.bfloat16)


def draw_cache_keys(key, part):
    collected_keys = jax.random.split(jax.random.fold_in(key, 41), 6)
    target_shape = (ALL_REQUEST_SLOTS, WINDOW_POSITIONS, KEY_VALUE_HEADS * HEAD_DIM)
    nearby_boundary = min(NEW_TOKENS, WINDOW_POSITIONS // 4)
    distant_boundary = WINDOW_POSITIONS // 2
    surge_width = min(32, WINDOW_POSITIONS // 8)
    slot_position = jnp.arange(WINDOW_POSITIONS)[None, :, None]
    surge_position = jax.random.randint(collected_keys[5], (ALL_REQUEST_SLOTS, 1, 1), nearby_boundary, distant_boundary - surge_width)
    inside_surge = (slot_position >= surge_position) & (slot_position < surge_position + surge_width)
    final_output = jnp.clip(jax.random.normal(collected_keys[0], target_shape, jnp.float32), -4.0, 4.0)
    final_output = jnp.where(inside_surge, 4.0 * final_output, final_output)
    return final_output.astype(jnp.bfloat16)


def levels(own_key, extent, cuts, low, top_value):
    level, own = 1.0, jax.random.fold_in(own_key, 6)
    for position, shards_of in cuts:
        draws = jnp.exp(jax.random.uniform(jax.random.fold_in(own, position), (shards_of,), jnp.float32, low / len(cuts), top_value / len(cuts)))
        level = level * jnp.repeat(draws, extent[position] // shards_of).reshape([-1 if axis == position else 1 for axis in range(len(extent))])
    return level


def centred(rng, shape, scale, most, cuts=(), kind=jnp.bfloat16):
    gain = levels(rng, shape, cuts, -0.22, 0.18) if cuts else 1.0
    result = jax.random.normal(rng, shape, jnp.float32) * scale * gain
    return jnp.minimum(jnp.maximum(result, -most), most).astype(kind)


def setup_inputs(seed: int = 0) -> dict:
    arg_keys = jax.random.split(jax.random.key(seed), 15)
    hidden_in = draw_hidden_in(jax.random.fold_in(arg_keys[14], 71), 0)
    cache_keys = draw_cache_keys(jax.random.fold_in(arg_keys[14], 71), 0)
    stored_cache_values = centred(arg_keys[2], (ALL_REQUEST_SLOTS, WINDOW_POSITIONS, KEY_VALUE_HEADS * HEAD_DIM), 1.0, 5.0, ((0, 16), (2, 2)))
    cache_lengths = draw_cache_lengths(jax.random.fold_in(arg_keys[14], 71), 0)
    live_slots = draw_live_slots(jax.random.fold_in(arg_keys[14], 71), 0)
    attn_gain = jnp.clip(1.0 + 0.18 * jax.random.normal(arg_keys[5], (MODEL_DIM,), jnp.float32), 0.1, 1.9)
    w_query = centred(arg_keys[6], (MODEL_DIM, QUERY_HEADS * HEAD_DIM), MODEL_DIM ** -0.5, 0.125, ((1, 2),))
    key_weight = centred(arg_keys[7], (MODEL_DIM, KEY_VALUE_HEADS * HEAD_DIM), MODEL_DIM ** -0.5, 0.125, ((1, 2),))
    value_weight = centred(arg_keys[8], (MODEL_DIM, KEY_VALUE_HEADS * HEAD_DIM), MODEL_DIM ** -0.5, 0.125, ((1, 2),))
    w_out = centred(arg_keys[9], (QUERY_HEADS * HEAD_DIM, MODEL_DIM), (QUERY_HEADS * HEAD_DIM) ** -0.5, 0.15625, ((0, 2),))
    mlp_gain = jnp.clip(1.0 + 0.18 * jax.random.normal(arg_keys[10], (MODEL_DIM,), jnp.float32), 0.1, 1.9)
    w_gate = centred(arg_keys[11], (MODEL_DIM, FFW), MODEL_DIM ** -0.5, 0.125, ((1, 2),))
    w_up = centred(arg_keys[12], (MODEL_DIM, FFW), MODEL_DIM ** -0.5, 0.125, ((1, 2),))
    w_down = centred(arg_keys[13], (FFW, MODEL_DIM), FFW ** -0.5, 0.09375, ((0, 2),))
    return dict(hidden_in=hidden_in, cache_keys=cache_keys, stored_cache_values=stored_cache_values, cache_lengths=cache_lengths, live_slots=live_slots, attn_gain=attn_gain, w_query=w_query, key_weight=key_weight, value_weight=value_weight, w_out=w_out, mlp_gain=mlp_gain, w_gate=w_gate, w_up=w_up, w_down=w_down)


EPSILON = 1e-05
ROPE_BASE = 10000.0

def rms_norm(values, norm_gain):
    widened = values.astype(jnp.float32)
    mean_square = lax.optimization_barrier(jnp.mean(widened * widened, axis=-1, keepdims=True))
    return widened * lax.rsqrt(mean_square + EPSILON) * norm_gain

def apply_rotary(values, token_positions):
    full_width = values.shape[-1]
    half_width = full_width // 2
    inverse = ROPE_BASE ** (-(jnp.arange(half_width, dtype=jnp.float32) * 2.0) / full_width)
    angles = token_positions.astype(jnp.float32)[..., None] * inverse
    cosine = jnp.cos(angles)[..., None, :]
    sine_part = jnp.sin(angles)[..., None, :]
    first_half = values[..., :half_width]
    second_half = values[..., half_width:]
    return jnp.concatenate([first_half * cosine - second_half * sine_part, second_half * cosine + first_half * sine_part], axis=-1)

def reference(hidden_in, cache_keys, stored_cache_values, cache_lengths, live_slots, attn_gain, w_query, key_weight, value_weight, w_out, mlp_gain, w_gate, w_up, w_down):
    query_group_count = QUERY_HEADS // KEY_VALUE_HEADS
    scaling = HEAD_DIM ** (-0.5)

    def one_slot(slot_items):
        tokens, cached_keys, cached_values, length, alive = slot_items
        normed = rms_norm(tokens, attn_gain).astype(jnp.bfloat16)
        queries = jnp.dot(normed, w_query, preferred_element_type=jnp.float32)
        incoming_keys = jnp.dot(normed, key_weight, preferred_element_type=jnp.float32)
        incoming_values = jnp.dot(normed, value_weight, preferred_element_type=jnp.float32)
        token_positions = length + jnp.arange(NEW_TOKENS, dtype=jnp.int32)
        queries = apply_rotary(queries.reshape(NEW_TOKENS, QUERY_HEADS, HEAD_DIM), token_positions).astype(jnp.bfloat16)
        incoming_keys = apply_rotary(incoming_keys.reshape(NEW_TOKENS, KEY_VALUE_HEADS, HEAD_DIM), token_positions).astype(jnp.bfloat16)
        incoming_values = incoming_values.astype(jnp.bfloat16).reshape(NEW_TOKENS, KEY_VALUE_HEADS, HEAD_DIM)
        key_pos = jnp.concatenate([length - WINDOW_POSITIONS + jnp.arange(WINDOW_POSITIONS, dtype=jnp.int32), token_positions])
        visible = (key_pos[None, :] >= 0) & (key_pos[None, :] <= token_positions[:, None]) & (token_positions[:, None] - key_pos[None, :] < WINDOW_POSITIONS)
        head_results = []
        for current_head_index in range(KEY_VALUE_HEADS):
            all_keys = jnp.concatenate([cached_keys[:, current_head_index * HEAD_DIM:(current_head_index + 1) * HEAD_DIM], incoming_keys[:, current_head_index, :]], axis=0)
            all_values = jnp.concatenate([cached_values[:, current_head_index * HEAD_DIM:(current_head_index + 1) * HEAD_DIM], incoming_values[:, current_head_index, :]], axis=0)
            head_queries = queries[:, current_head_index * query_group_count:(current_head_index + 1) * query_group_count, :]
            scores = jnp.einsum('tgd,ud->tgu', head_queries.astype(jnp.float32), all_keys.astype(jnp.float32)) * scaling
            scores = jnp.where(visible[:, None, :], scores, -jnp.inf)
            top = lax.optimization_barrier(jnp.max(scores, axis=-1, keepdims=True))
            raised = jnp.exp(scores - top)
            mass = lax.optimization_barrier(jnp.sum(raised, axis=-1, keepdims=True))
            weights = (raised / mass).astype(jnp.bfloat16)
            head_results.append(jnp.einsum('tgu,ud->tgd', weights.astype(jnp.float32), all_values.astype(jnp.float32)))
        attended = jnp.stack(head_results, axis=1).reshape(NEW_TOKENS, QUERY_HEADS * HEAD_DIM).astype(jnp.bfloat16)
        residual = (tokens.astype(jnp.float32) + jnp.dot(attended, w_out, preferred_element_type=jnp.float32)).astype(jnp.bfloat16)
        mlp_in = rms_norm(residual, mlp_gain).astype(jnp.bfloat16)
        gate_part = jnp.dot(mlp_in, w_gate, preferred_element_type=jnp.float32)
        up_part = jnp.dot(mlp_in, w_up, preferred_element_type=jnp.float32)
        activated = (jax.nn.silu(gate_part) * up_part).astype(jnp.bfloat16)
        completed_output = (residual.astype(jnp.float32) + jnp.dot(activated, w_down, preferred_element_type=jnp.float32)).astype(jnp.bfloat16)
        window_mask = alive > 0
        empty_value_rows = jnp.zeros((), jnp.bfloat16)
        return (jnp.where(window_mask, completed_output, empty_value_rows), jnp.where(window_mask, incoming_keys.reshape(NEW_TOKENS, KEY_VALUE_HEADS * HEAD_DIM), empty_value_rows), jnp.where(window_mask, incoming_values.reshape(NEW_TOKENS, KEY_VALUE_HEADS * HEAD_DIM), empty_value_rows))
    hidden_out, new_keys, new_values = lax.map(one_slot, (hidden_in, cache_keys, stored_cache_values, cache_lengths, live_slots))
    return (hidden_out, new_keys, new_values)
```

```python
import functools

import jax
import jax.numpy as jnp
from jax import lax
from jax.experimental import pallas as pl
from jax.experimental.pallas import tpu as pltpu
from jax.sharding import PartitionSpec as P

HEAD_DIM = 80
EPSILON = 1e-05
ROPE_BASE = 10000.0
LOG2E = 1.4426950408889634
KEY_BLOCK = 512
NT = (((1,), (1,)), ((), ()))


def attention_kernel(
    kv_heads,
    group,
    scal_ref,
    own_ref,
    other_ref,
    gain_ref,
    wq_ref,
    wk_ref,
    wv_ref,
    cos_ref,
    sin_ref,
    k_ref,
    v_ref,
    att_ref,
    nk_ref,
    nv_ref,
    nrm,
    q_s,
    kf_s,
    kpad,
    v_s,
    acc,
    top,
):
    heads = kv_heads * group
    half = own_ref.shape[0]
    rows = 2 * half
    window = k_ref.shape[0]
    kw = kv_heads * HEAD_DIM
    wide = acc.shape[2]
    qw = heads * HEAD_DIM
    length = scal_ref[0]
    alive = scal_ref[1]
    tok = scal_ref[2]
    scale = (HEAD_DIM**-0.5) * LOG2E

    @pl.when(alive == 0)
    def _():
        att_ref[...] = jnp.zeros_like(att_ref)
        nk_ref[...] = jnp.zeros_like(nk_ref)
        nv_ref[...] = jnp.zeros_like(nv_ref)

    @pl.when(alive > 0)
    def _():
        for part, ref in enumerate((own_ref, other_ref)):
            x = ref[...].astype(jnp.float32)
            ms = jnp.mean(x * x, axis=1, keepdims=True)
            nrm[part * half : (part + 1) * half, :] = (
                x * lax.rsqrt(ms + EPSILON) * gain_ref[...]
            ).astype(jnp.bfloat16)
        normed = nrm[...]
        x = jnp.dot(normed, wq_ref[...], preferred_element_type=jnp.float32)
        lane = lax.broadcasted_iota(jnp.int32, (rows, qw), 1)
        first = lax.rem(lane, HEAD_DIM) < HEAD_DIM // 2
        turned = jnp.where(
            first, pltpu.roll(x, qw - HEAD_DIM // 2, 1), pltpu.roll(x, HEAD_DIM // 2, 1)
        )
        q = x * cos_ref[...] + turned * sin_ref[...]
        lane2 = lax.broadcasted_iota(jnp.int32, (rows, wide), 1)
        for h in range(heads):
            g = h // group
            shift = (g * HEAD_DIM - h * HEAD_DIM) % qw
            r = q if shift == 0 else pltpu.roll(q, shift, 1)
            r = r[:, :wide]
            keep = (lane2 >= g * HEAD_DIM) & (lane2 < (g + 1) * HEAD_DIM)
            q_s[h] = jnp.where(keep, r, 0.0).astype(jnp.bfloat16)[:, :kw]
        kpad[...] = jnp.zeros_like(kpad)
        kpad[:, :kw] = jnp.dot(normed, wk_ref[...], preferred_element_type=jnp.float32)
        x = kpad[...]
        turned = jnp.where(
            lax.rem(lane2, HEAD_DIM) < HEAD_DIM // 2,
            pltpu.roll(x, wide - HEAD_DIM // 2, 1),
            pltpu.roll(x, HEAD_DIM // 2, 1),
        )
        fresh_k = (x * cos_ref[:, :wide] + turned * sin_ref[:, :wide]).astype(jnp.bfloat16)[:, :kw]
        kf_s[...] = fresh_k
        fresh_v = jnp.dot(normed, wv_ref[...], preferred_element_type=jnp.float32).astype(
            jnp.bfloat16
        )
        v_s[...] = jnp.ones_like(v_s)
        v_s[:window, :kw] = v_ref[...]
        v_s[window:, :kw] = fresh_v
        for part in range(2):
            start = pl.multiple_of((tok if part == 0 else 1 - tok) * half, half)
            nk_ref[pl.ds(start, half), :] = fresh_k[part * half : (part + 1) * half]
            nv_ref[pl.ds(start, half), :] = fresh_v[part * half : (part + 1) * half]

        def token_of(index):
            return index + jnp.where(index < half, tok * half, -tok * half)

        row_t = token_of(lax.broadcasted_iota(jnp.int32, (rows, rows), 0))
        col_t = token_of(lax.broadcasted_iota(jnp.int32, (rows, rows), 1))
        seen = col_t <= row_t
        keys = kf_s[...]
        vals = v_s[window:, :]
        for h in range(heads):
            s = lax.dot_general(q_s[h], keys, NT, preferred_element_type=jnp.float32) * scale
            s = jnp.where(seen, s, -jnp.inf)
            m = jnp.broadcast_to(jnp.max(s, axis=1, keepdims=True), (rows, 128))
            p = jnp.exp2(s - jnp.concatenate([m] * (rows // 128), axis=1))
            top[h] = m
            acc[h] = jnp.dot(p.astype(jnp.bfloat16), vals, preferred_element_type=jnp.float32)

        def block(index, masked):
            start = pl.multiple_of(index * KEY_BLOCK, KEY_BLOCK)
            keys = k_ref[pl.ds(start, KEY_BLOCK), :]
            vals = v_s[pl.ds(start, KEY_BLOCK), :]
            if masked:
                row_t = token_of(lax.broadcasted_iota(jnp.int32, (rows, KEY_BLOCK), 0))
                col = start + lax.broadcasted_iota(jnp.int32, (rows, KEY_BLOCK), 1)
                seen = (col > row_t) & (col >= window - length)
            for h in range(heads):
                s = lax.dot_general(q_s[h], keys, NT, preferred_element_type=jnp.float32) * scale
                if masked:
                    s = jnp.where(seen, s, -jnp.inf)
                old = top[h]
                m = jnp.maximum(old, jnp.max(s, axis=1, keepdims=True))
                p = jnp.exp2(s - jnp.concatenate([m] * (KEY_BLOCK // 128), axis=1))
                alpha = jnp.exp2(old - m)
                top[h] = m
                acc[h] = acc[h] * jnp.concatenate([alpha] * (wide // 128), axis=1) + jnp.dot(
                    p.astype(jnp.bfloat16), vals, preferred_element_type=jnp.float32
                )

        blocks = window // KEY_BLOCK
        first_block = jnp.maximum(window - length, 0) // KEY_BLOCK

        @pl.when(first_block < blocks)
        def _():
            block(first_block, True)

        @pl.loop(first_block + 1, blocks)
        def _(index):
            block(index, False)

        total = jnp.zeros((rows, qw), jnp.float32)
        for h in range(heads):
            g = h // group
            a = acc[h]
            o = a / a[:, kw : kw + 1]
            keep = (lane2 >= g * HEAD_DIM) & (lane2 < (g + 1) * HEAD_DIM)
            o = jnp.where(keep, o, 0.0)
            o = jnp.concatenate([o, jnp.zeros((rows, qw - wide), jnp.float32)], axis=1)
            shift = (h * HEAD_DIM - g * HEAD_DIM) % qw
            total = total + (o if shift == 0 else pltpu.roll(o, shift, 1))
        att_ref[...] = total.astype(jnp.bfloat16)


def attention(slot, scal, own, other, gain, wq, wk, wv, cos, sin, keys, values):
    half, width = own.shape
    rows = 2 * half
    qw, kw = wq.shape[1], wk.shape[1]
    heads, kv_heads = qw // HEAD_DIM, kw // HEAD_DIM
    window = keys.shape[1]
    wide = -(-(kw + 1) // 128) * 128
    whole = lambda a: pl.BlockSpec(a.shape, lambda i, s: (0,) * a.ndim)
    of_slot = lambda a: pl.BlockSpec(
        (None,) + a.shape[1:], lambda i, s: (slot,) + (0,) * (a.ndim - 1)
    )
    out = lambda w: (jax.ShapeDtypeStruct((rows, w), jnp.bfloat16))
    return pl.pallas_call(
        functools.partial(attention_kernel, kv_heads, heads // kv_heads),
        grid_spec=pltpu.PrefetchScalarGridSpec(
            num_scalar_prefetch=1,
            grid=(1,),
            in_specs=[
                whole(own),
                whole(other),
                whole(gain),
                whole(wq),
                whole(wk),
                whole(wv),
                of_slot(cos),
                of_slot(sin),
                of_slot(keys),
                of_slot(values),
            ],
            out_specs=[
                pl.BlockSpec((rows, w), lambda i, s: (0, 0)) for w in (qw, kw, kw)
            ],
            scratch_shapes=[
                pltpu.VMEM((rows, width), jnp.bfloat16),
                pltpu.VMEM((heads, rows, kw), jnp.bfloat16),
                pltpu.VMEM((rows, kw), jnp.bfloat16),
                pltpu.VMEM((rows, wide), jnp.float32),
                pltpu.VMEM((window + rows, wide), jnp.bfloat16),
                pltpu.VMEM((heads, rows, wide), jnp.float32),
                pltpu.VMEM((heads, rows, 128), jnp.float32),
            ],
        ),
        out_shape=[out(qw), out(kw), out(kw)],
        compiler_params=pltpu.CompilerParams(vmem_limit_bytes=48 * 1024 * 1024),
        cost_estimate=pl.CostEstimate(
            flops=12 * 10**9, bytes_accessed=12 * 10**6, transcendentals=9 * 10**6
        ),
        name="attention",
    )(scal, own, other, gain, wq, wk, wv, cos, sin, keys, values)


def local(
    hidden_in,
    cache_keys,
    stored_cache_values,
    cache_lengths,
    live_slots,
    attn_gain,
    w_query,
    key_weight,
    value_weight,
    w_out,
    mlp_gain,
    w_gate,
    w_up,
    w_down,
):
    slots, half, width = hidden_in.shape
    rows = 2 * half
    qw = w_query.shape[1]
    tok = lax.axis_index("tok")
    req = lax.axis_index("req")
    reqs = lax.axis_size("req")
    swap = [(0, 1), (1, 0)]
    other_half = lambda a: lax.ppermute(a, "tok", swap)

    others = [other_half(hidden_in[s]) for s in range(slots)]
    share = w_out.shape[0] // reqs
    piece = lax.dynamic_slice_in_dim(w_out, req * share, share, 0)
    w_other = lax.all_gather(other_half(piece), "req", axis=0, tiled=True)

    alive = lax.dynamic_slice_in_dim(live_slots, req * slots, slots)
    index = jnp.arange(rows, dtype=jnp.int32)
    token = index + jnp.where(index < half, tok * half, -tok * half)
    positions = cache_lengths[:, None] + token[None, :]
    h2 = HEAD_DIM // 2
    inverse = ROPE_BASE ** (-(jnp.arange(h2, dtype=jnp.float32) * 2.0) / HEAD_DIM)
    angles = positions.astype(jnp.float32)[..., None] * inverse
    c, s_ = jnp.cos(angles), jnp.sin(angles)
    cos = jnp.tile(jnp.concatenate([c, c], axis=-1), (1, 1, qw // HEAD_DIM))
    sin = jnp.tile(jnp.concatenate([-s_, s_], axis=-1), (1, 1, qw // HEAD_DIM))

    attended = []
    new_keys = []
    new_values = []
    for s in range(slots):
        scal = jnp.stack([cache_lengths[s], alive[s], tok.astype(jnp.int32)])
        a, k, v = attention(
            s,
            scal,
            hidden_in[s],
            others[s],
            attn_gain[None, :],
            w_query,
            key_weight,
            value_weight,
            cos,
            sin,
            cache_keys,
            stored_cache_values,
        )
        attended.append(a)
        new_keys.append(k)
        new_values.append(v)
    results = []
    for s in range(slots):
        a = attended[s]
        b = other_half(a)
        b = jnp.concatenate([b[half:], b[:half]], axis=0)
        hid = jnp.concatenate([hidden_in[s], others[s]], axis=0).astype(jnp.float32)
        residual = (
            hid
            + jnp.dot(a, w_out, preferred_element_type=jnp.float32)
            + jnp.dot(b, w_other, preferred_element_type=jnp.float32)
        ).astype(jnp.bfloat16)
        wide = residual.astype(jnp.float32)
        ms = jnp.mean(wide * wide, axis=-1, keepdims=True)
        mlp_in = (wide * lax.rsqrt(ms + EPSILON) * mlp_gain).astype(jnp.bfloat16)
        gate = jnp.dot(mlp_in, w_gate, preferred_element_type=jnp.float32)
        up = jnp.dot(mlp_in, w_up, preferred_element_type=jnp.float32)
        act = (jax.nn.silu(gate) * up).astype(jnp.bfloat16)
        sent = other_half(
            jnp.dot(act[half:], w_down, preferred_element_type=jnp.float32).astype(jnp.bfloat16)
        )
        mine = jnp.dot(act[:half], w_down, preferred_element_type=jnp.float32)
        out = wide[:half] + mine + sent.astype(jnp.float32)
        out = jnp.where(alive[s] > 0, out, 0.0).astype(jnp.bfloat16)
        results.append(out)
    return (jnp.stack(results), jnp.stack(new_keys), jnp.stack(new_values))


def solution(mesh):
    return jax.shard_map(
        local,
        mesh=mesh,
        in_specs=(
            P("req", "tok", None),
            P("req", None, "tok"),
            P("req", None, "tok"),
            P("req"),
            P(),
            P(),
            P(None, "tok"),
            P(None, "tok"),
            P(None, "tok"),
            P("tok", None),
            P(),
            P(None, "tok"),
            P(None, "tok"),
            P("tok", None),
        ),
        out_specs=(P("req", "tok", None), P("req", None, "tok"), P("req", None, "tok")),
        check_vma=False,
    )
```

```python
import functools

import jax
import jax.numpy as jnp
from jax import lax
from jax.experimental import pallas as pl
from jax.experimental.pallas import tpu as pltpu
from jax.sharding import PartitionSpec as P

HEAD_DIM = 80
EPSILON = 1e-05
ROPE_BASE = 10000.0
LOG2E = 1.4426950408889634
KEY_BLOCK = 512
ROW_CHUNK = 512
HIDDEN_CHUNK = 256
NT = (((1,), (1,)), ((), ()))


def attention_kernel(
    kv_heads,
    group,
    slot,
    scal_ref,
    own_ref,
    other_ref,
    gain_ref,
    cos_ref,
    sin_ref,
    wq_hbm,
    wk_hbm,
    wv_hbm,
    k_hbm,
    v_hbm,
    att_ref,
    nk_ref,
    nv_ref,
    nrm,
    q_s,
    wq_ref,
    wk_ref,
    wv_ref,
    k_ref,
    v_ref,
    acc,
    top,
    sems,
):
    heads = kv_heads * group
    half = own_ref.shape[0]
    rows = 2 * half
    kw, window = k_ref.shape
    wide = acc.shape[2]
    qw = heads * HEAD_DIM
    h2 = HEAD_DIM // 2
    length = scal_ref[0]
    alive = scal_ref[1]
    tok = scal_ref[2]
    scale = (HEAD_DIM**-0.5) * LOG2E

    @pl.when(alive == 0)
    def _():
        att_ref[...] = jnp.zeros_like(att_ref)
        nk_ref[...] = jnp.zeros_like(nk_ref)
        nv_ref[...] = jnp.zeros_like(nv_ref)

    @pl.when(alive > 0)
    def _():
        copies = [
            pltpu.make_async_copy(src, dst, sems.at[i])
            for i, (src, dst) in enumerate(
                (
                    (wq_hbm, wq_ref),
                    (wk_hbm, wk_ref),
                    (wv_hbm, wv_ref),
                    (k_hbm.at[slot], k_ref),
                    (v_hbm.at[slot], v_ref),
                )
            )
        ]
        for copy in copies:
            copy.start()
        for part, ref in enumerate((own_ref, other_ref)):
            x = ref[...].astype(jnp.float32)
            ms = jnp.mean(x * x, axis=1, keepdims=True)
            nrm[part * half : (part + 1) * half, :] = (
                x * lax.rsqrt(ms + EPSILON) * gain_ref[...]
            ).astype(jnp.bfloat16)
        cos_t, sin_t = cos_ref[...], sin_ref[...]
        cos = jnp.concatenate([cos_t, cos_t] * heads, axis=0).T
        sin = jnp.concatenate([-sin_t, sin_t] * heads, axis=0).T
        normed = nrm[...]
        copies[0].wait()
        x = jnp.dot(normed, wq_ref[...], preferred_element_type=jnp.float32)
        lane = lax.broadcasted_iota(jnp.int32, (rows, qw), 1)
        turned = jnp.where(
            lax.rem(lane, HEAD_DIM) < h2, pltpu.roll(x, qw - h2, 1), pltpu.roll(x, h2, 1)
        )
        q = x * cos + turned * sin
        lane2 = lax.broadcasted_iota(jnp.int32, (rows, wide), 1)
        for h in range(heads):
            g = h // group
            shift = (g * HEAD_DIM - h * HEAD_DIM) % qw
            r = q if shift == 0 else pltpu.roll(q, shift, 1)
            r = r[:, :wide]
            keep = (lane2 >= g * HEAD_DIM) & (lane2 < (g + 1) * HEAD_DIM)
            q_s[h] = jnp.where(keep, r, 0.0).astype(jnp.bfloat16)[:, :kw]
        copies[1].wait()
        x = lax.dot_general(wk_ref[...], normed, NT, preferred_element_type=jnp.float32)
        turned = []
        for g in range(kv_heads):
            a = x[g * HEAD_DIM : g * HEAD_DIM + h2]
            b = x[g * HEAD_DIM + h2 : (g + 1) * HEAD_DIM]
            turned += [a * cos_t - b * sin_t, b * cos_t + a * sin_t]
        fresh_k = jnp.concatenate(turned, axis=0).astype(jnp.bfloat16)
        copies[2].wait()
        fresh_v = lax.dot_general(
            wv_ref[...], normed, NT, preferred_element_type=jnp.float32
        ).astype(jnp.bfloat16)
        for part in range(2):
            start = pl.multiple_of((tok if part == 0 else 1 - tok) * half, half)
            nk_ref[:, pl.ds(start, half)] = fresh_k[:, part * half : (part + 1) * half]
            nv_ref[:, pl.ds(start, half)] = fresh_v[:, part * half : (part + 1) * half]

        def token_of(index):
            return index + jnp.where(index < half, tok * half, -tok * half)

        def with_ones(vals):
            return jnp.concatenate(
                [vals, jnp.ones((wide - kw, vals.shape[1]), jnp.bfloat16)], axis=0
            )

        row_t = token_of(lax.broadcasted_iota(jnp.int32, (rows, rows), 0))
        col_t = token_of(lax.broadcasted_iota(jnp.int32, (rows, rows), 1))
        seen = col_t <= row_t
        vals = with_ones(fresh_v)
        for h in range(heads):
            s = jnp.dot(q_s[h], fresh_k, preferred_element_type=jnp.float32) * scale
            s = jnp.where(seen, s, -jnp.inf)
            m = jnp.broadcast_to(jnp.max(s, axis=1, keepdims=True), (rows, 128))
            p = jnp.exp2(s - jnp.concatenate([m] * (rows // 128), axis=1))
            top[h] = m
            acc[h] = lax.dot_general(
                p.astype(jnp.bfloat16), vals, NT, preferred_element_type=jnp.float32
            )

        def block(index, masked):
            start = pl.multiple_of(index * KEY_BLOCK, KEY_BLOCK)
            keys = k_ref[:, pl.ds(start, KEY_BLOCK)]
            vals = with_ones(v_ref[:, pl.ds(start, KEY_BLOCK)])
            if masked:
                row_t = token_of(lax.broadcasted_iota(jnp.int32, (rows, KEY_BLOCK), 0))
                col = start + lax.broadcasted_iota(jnp.int32, (rows, KEY_BLOCK), 1)
                seen = (col > row_t) & (col >= window - length)
            for h in range(heads):
                s = jnp.dot(q_s[h], keys, preferred_element_type=jnp.float32) * scale
                if masked:
                    s = jnp.where(seen, s, -jnp.inf)
                old = top[h]
                m = jnp.maximum(old, jnp.max(s, axis=1, keepdims=True))
                p = jnp.exp2(s - jnp.concatenate([m] * (KEY_BLOCK // 128), axis=1))
                alpha = jnp.exp2(old - m)
                top[h] = m
                acc[h] = acc[h] * jnp.concatenate(
                    [alpha] * (wide // 128), axis=1
                ) + lax.dot_general(
                    p.astype(jnp.bfloat16), vals, NT, preferred_element_type=jnp.float32
                )

        blocks = window // KEY_BLOCK
        first_block = jnp.maximum(window - length, 0) // KEY_BLOCK
        copies[3].wait()
        copies[4].wait()

        @pl.when(first_block < blocks)
        def _():
            block(first_block, True)

        @pl.loop(first_block + 1, blocks)
        def _(index):
            block(index, False)

        total = jnp.zeros((rows, qw), jnp.float32)
        for h in range(heads):
            g = h // group
            a = acc[h]
            o = a / a[:, kw : kw + 1]
            keep = (lane2 >= g * HEAD_DIM) & (lane2 < (g + 1) * HEAD_DIM)
            o = jnp.where(keep, o, 0.0)
            o = jnp.concatenate([o, jnp.zeros((rows, qw - wide), jnp.float32)], axis=1)
            shift = (h * HEAD_DIM - g * HEAD_DIM) % qw
            total = total + (o if shift == 0 else pltpu.roll(o, shift, 1))
        att_ref[...] = total.astype(jnp.bfloat16)


def whole(a):
    return pl.BlockSpec(a.shape, lambda *_: (0,) * a.ndim)


def of_slot(slot, a):
    return pl.BlockSpec((None,) + a.shape[1:], lambda *_: (slot,) + (0,) * (a.ndim - 1))


ANY = pl.BlockSpec(memory_space=pl.ANY)


def attention(slot, scal, hidden, other, gain, cos, sin, wq, wk_t, wv_t, keys_t, values_t):
    half, width = other.shape
    rows = 2 * half
    qw, kw = wq.shape[1], wk_t.shape[0]
    heads, kv_heads = qw // HEAD_DIM, kw // HEAD_DIM
    window = keys_t.shape[2]
    wide = -(-(kw + 1) // 128) * 128
    shapes = [(rows, qw), (kw, rows), (kw, rows)]
    bf16 = jnp.bfloat16
    return pl.pallas_call(
        functools.partial(attention_kernel, kv_heads, heads // kv_heads, slot),
        grid_spec=pltpu.PrefetchScalarGridSpec(
            num_scalar_prefetch=1,
            grid=(1,),
            in_specs=[
                of_slot(slot, hidden),
                whole(other),
                whole(gain),
                of_slot(slot, cos),
                of_slot(slot, sin),
            ]
            + [ANY] * 5,
            out_specs=[pl.BlockSpec(s, lambda *_: (0, 0)) for s in shapes],
            scratch_shapes=[
                pltpu.VMEM((rows, width), bf16),
                pltpu.VMEM((heads, rows, kw), bf16),
                pltpu.VMEM(wq.shape, bf16),
                pltpu.VMEM(wk_t.shape, bf16),
                pltpu.VMEM(wv_t.shape, bf16),
                pltpu.VMEM((kw, window), bf16),
                pltpu.VMEM((kw, window), bf16),
                pltpu.VMEM((heads, rows, wide), jnp.float32),
                pltpu.VMEM((heads, rows, 128), jnp.float32),
                pltpu.SemaphoreType.DMA((5,)),
            ],
        ),
        out_shape=[jax.ShapeDtypeStruct(s, bf16) for s in shapes],
        compiler_params=pltpu.CompilerParams(vmem_limit_bytes=40 * 1024 * 1024),
        cost_estimate=pl.CostEstimate(
            flops=20 * 10**9, bytes_accessed=10 * 10**6, transcendentals=9 * 10**6
        ),
        name="attention",
    )(scal, hidden, other, gain, cos, sin, wq, wk_t, wv_t, keys_t, values_t)


def mlp_kernel(
    scal_ref,
    a_ref,
    b_ref,
    own_ref,
    other_ref,
    gain_ref,
    wo_hbm,
    got_hbm,
    sib_hbm,
    wg_ref,
    wu_ref,
    wd_ref,
    mine_ref,
    theirs_ref,
    w_s,
    res,
    nrm,
    acc,
    sems,
):
    step = pl.program_id(0)
    half, width = own_ref.shape
    depth = wo_hbm.shape[0]
    part_rows = got_hbm.shape[0]
    core = scal_ref[0]

    @pl.when(step == 0)
    def _():
        copies = [
            pltpu.make_async_copy(wo_hbm, w_s.at[0], sems.at[0]),
            pltpu.make_async_copy(
                got_hbm,
                w_s.at[1, pl.ds(pl.multiple_of(core * part_rows, part_rows), part_rows)],
                sems.at[1],
            ),
            pltpu.make_async_copy(
                sib_hbm,
                w_s.at[1, pl.ds(pl.multiple_of((1 - core) * part_rows, part_rows), part_rows)],
                sems.at[2],
            ),
        ]
        for copy in copies:
            copy.start()
        for copy in copies:
            copy.wait()
        a = a_ref[...]
        b = jnp.concatenate([b_ref[half:, :], b_ref[:half, :]], axis=0)
        square = jnp.zeros((2 * half, 1), jnp.float32)
        for c in range(0, width, ROW_CHUNK):
            cols = slice(c, c + ROW_CHUNK)
            r = jnp.dot(a, w_s[0, :, cols], preferred_element_type=jnp.float32)
            r = r + jnp.dot(b, w_s[1, :, cols], preferred_element_type=jnp.float32)
            hid = jnp.concatenate([own_ref[:, cols], other_ref[:, cols]], axis=0)
            r = (r + hid.astype(jnp.float32)).astype(jnp.bfloat16)
            res[:, cols] = r
            r = r.astype(jnp.float32)
            square = square + jnp.sum(r * r, axis=1, keepdims=True)
        inv = lax.rsqrt(square / width + EPSILON)
        for c in range(0, width, ROW_CHUNK):
            cols = slice(c, c + ROW_CHUNK)
            r = res[:, cols].astype(jnp.float32)
            nrm[:, cols] = (r * inv * gain_ref[:, cols]).astype(jnp.bfloat16)

    x = nrm[...]
    gate = jnp.dot(x, wg_ref[...], preferred_element_type=jnp.float32)
    up = jnp.dot(x, wu_ref[...], preferred_element_type=jnp.float32)
    act = (gate / (1.0 + jnp.exp(-gate)) * up).astype(jnp.bfloat16)
    for c in range(0, width, ROW_CHUNK):
        cols = slice(c, c + ROW_CHUNK)
        part = jnp.dot(act, wd_ref[:, cols], preferred_element_type=jnp.float32)

        @pl.when(step == 0)
        def _():
            acc[:, cols] = part

        @pl.when(step > 0)
        def _():
            acc[:, cols] += part

    @pl.when(step == pl.num_programs(0) - 1)
    def _():
        mine_ref[...] = acc[:half, :] + res[:half, :].astype(jnp.float32)
        theirs_ref[...] = acc[half:, :].astype(jnp.bfloat16)


def mlp(slot, scal, a, b, hidden, other, gain, w_out, got, sib, w_gate, w_up, w_down):
    half, width = other.shape
    rows = 2 * half
    ffw = w_gate.shape[1]
    bf16 = jnp.bfloat16
    return pl.pallas_call(
        mlp_kernel,
        grid_spec=pltpu.PrefetchScalarGridSpec(
            num_scalar_prefetch=1,
            grid=(ffw // HIDDEN_CHUNK,),
            in_specs=[whole(a), whole(b), of_slot(slot, hidden), whole(other), whole(gain)]
            + [ANY] * 3
            + [
                pl.BlockSpec((width, HIDDEN_CHUNK), lambda j, s: (0, j)),
                pl.BlockSpec((width, HIDDEN_CHUNK), lambda j, s: (0, j)),
                pl.BlockSpec((HIDDEN_CHUNK, width), lambda j, s: (j, 0)),
            ],
            out_specs=[pl.BlockSpec((half, width), lambda *_: (0, 0))] * 2,
            scratch_shapes=[
                pltpu.VMEM((2,) + w_out.shape, bf16),
                pltpu.VMEM((rows, width), bf16),
                pltpu.VMEM((rows, width), bf16),
                pltpu.VMEM((rows, width), jnp.float32),
                pltpu.SemaphoreType.DMA((3,)),
            ],
        ),
        out_shape=[
            jax.ShapeDtypeStruct((half, width), jnp.float32),
            jax.ShapeDtypeStruct((half, width), bf16),
        ],
        compiler_params=pltpu.CompilerParams(vmem_limit_bytes=48 * 1024 * 1024),
        cost_estimate=pl.CostEstimate(
            flops=9 * 10**9, bytes_accessed=36 * 10**6, transcendentals=10**6
        ),
        name="mlp",
    )(scal, a, b, hidden, other, gain, w_out, got, sib, w_gate, w_up, w_down)


def local(
    hidden_in,
    cache_keys,
    stored_cache_values,
    cache_lengths,
    live_slots,
    attn_gain,
    w_query,
    key_weight,
    value_weight,
    w_out,
    mlp_gain,
    w_gate,
    w_up,
    w_down,
):
    slots, half, width = hidden_in.shape
    rows = 2 * half
    tok = lax.axis_index("tok").astype(jnp.int32)
    req = lax.axis_index("req").astype(jnp.int32)
    reqs = lax.axis_size("req")
    swap = [(0, 1), (1, 0)]
    other_half = lambda a: lax.ppermute(a, "tok", swap)

    others = [other_half(hidden_in[s]) for s in range(slots)]
    core = lax.rem(req, 2)
    share = w_out.shape[0] // 2
    got = other_half(lax.dynamic_slice_in_dim(w_out, core * share, share, 0))
    sib = lax.ppermute(got, "req", [(i, i ^ 1) for i in range(reqs)])

    alive = lax.dynamic_slice_in_dim(live_slots, req * slots, slots)
    index = jnp.arange(rows, dtype=jnp.int32)
    token = index + jnp.where(index < half, tok * half, -tok * half)
    positions = cache_lengths[:, None] + token[None, :]
    h2 = HEAD_DIM // 2
    inverse = ROPE_BASE ** (-(jnp.arange(h2, dtype=jnp.float32) * 2.0) / HEAD_DIM)
    angles = positions.astype(jnp.float32)[:, None, :] * inverse[None, :, None]
    cos, sin = jnp.cos(angles), jnp.sin(angles)

    flip = lambda a: jnp.swapaxes(a, -1, -2)
    keys_t, values_t = flip(cache_keys), flip(stored_cache_values)
    wk_t, wv_t = flip(key_weight), flip(value_weight)
    attended = []
    new_keys = []
    new_values = []
    for s in range(slots):
        scal = jnp.stack([cache_lengths[s], alive[s], tok])
        a, k, v = attention(
            s,
            scal,
            hidden_in,
            others[s],
            attn_gain[None, :],
            cos,
            sin,
            w_query,
            wk_t,
            wv_t,
            keys_t,
            values_t,
        )
        attended.append(a)
        new_keys.append(k)
        new_values.append(v)
    received = [other_half(a) for a in attended]
    results = []
    for s in range(slots):
        mine, theirs = mlp(
            s,
            core[None],
            attended[s],
            received[s],
            hidden_in,
            others[s],
            mlp_gain[None, :],
            w_out,
            got,
            sib,
            w_gate,
            w_up,
            w_down,
        )
        out = mine + other_half(theirs).astype(jnp.float32)
        results.append(jnp.where(alive[s] > 0, out, 0.0).astype(jnp.bfloat16))
    return (jnp.stack(results), flip(jnp.stack(new_keys)), flip(jnp.stack(new_values)))


def solution(mesh):
    return jax.shard_map(
        local,
        mesh=mesh,
        in_specs=(
            P("req", "tok", None),
            P("req", None, "tok"),
            P("req", None, "tok"),
            P("req"),
            P(),
            P(),
            P(None, "tok"),
            P(None, "tok"),
            P(None, "tok"),
            P("tok", None),
            P(),
            P(None, "tok"),
            P(None, "tok"),
            P("tok", None),
        ),
        out_specs=(P("req", "tok", None), P("req", None, "tok"), P("req", None, "tok")),
        check_vma=False,
    )
```

```python
import functools

import jax
import jax.numpy as jnp
from jax import lax
from jax.experimental import pallas as pl
from jax.experimental.pallas import tpu as pltpu
from jax.sharding import PartitionSpec as P

HEAD_DIM = 80
EPSILON = 1e-05
ROPE_BASE = 10000.0
LOG2E = 1.4426950408889634
KEY_BLOCK = 512
ROW_CHUNK = 512
NT = (((1,), (1,)), ((), ()))


def attention_kernel(
    kv_heads,
    group,
    slot,
    scal_ref,
    own_ref,
    other_ref,
    gain_ref,
    cos_ref,
    sin_ref,
    wq_hbm,
    wk_hbm,
    wv_hbm,
    k_hbm,
    v_hbm,
    att_ref,
    nk_ref,
    nv_ref,
    nrm,
    q_s,
    wq_ref,
    wk_ref,
    wv_ref,
    k_ref,
    v_ref,
    acc,
    top,
    sems,
):
    heads = kv_heads * group
    half = own_ref.shape[0]
    rows = 2 * half
    kw, window = k_ref.shape
    wide = acc.shape[2]
    qw = heads * HEAD_DIM
    h2 = HEAD_DIM // 2
    length = scal_ref[0]
    alive = scal_ref[1]
    tok = scal_ref[2]
    scale = (HEAD_DIM**-0.5) * LOG2E

    @pl.when(alive == 0)
    def _():
        att_ref[...] = jnp.zeros_like(att_ref)
        nk_ref[...] = jnp.zeros_like(nk_ref)
        nv_ref[...] = jnp.zeros_like(nv_ref)

    @pl.when(alive > 0)
    def _():
        copies = [
            pltpu.make_async_copy(src, dst, sems.at[i])
            for i, (src, dst) in enumerate(
                (
                    (wq_hbm, wq_ref),
                    (wk_hbm, wk_ref),
                    (wv_hbm, wv_ref),
                    (k_hbm.at[slot], k_ref),
                    (v_hbm.at[slot], v_ref),
                )
            )
        ]
        for copy in copies:
            copy.start()
        for part, ref in enumerate((own_ref, other_ref)):
            x = ref[...].astype(jnp.float32)
            ms = jnp.mean(x * x, axis=1, keepdims=True)
            nrm[part * half : (part + 1) * half, :] = (
                x * lax.rsqrt(ms + EPSILON) * gain_ref[...]
            ).astype(jnp.bfloat16)
        cos_t, sin_t = cos_ref[...], sin_ref[...]
        cos = jnp.concatenate([cos_t, cos_t] * heads, axis=0).T
        sin = jnp.concatenate([-sin_t, sin_t] * heads, axis=0).T
        normed = nrm[...]
        copies[0].wait()
        x = jnp.dot(normed, wq_ref[...], preferred_element_type=jnp.float32)
        lane = lax.broadcasted_iota(jnp.int32, (rows, qw), 1)
        turned = jnp.where(
            lax.rem(lane, HEAD_DIM) < h2, pltpu.roll(x, qw - h2, 1), pltpu.roll(x, h2, 1)
        )
        q = x * cos + turned * sin
        lane2 = lax.broadcasted_iota(jnp.int32, (rows, wide), 1)
        for h in range(heads):
            g = h // group
            shift = (g * HEAD_DIM - h * HEAD_DIM) % qw
            r = q if shift == 0 else pltpu.roll(q, shift, 1)
            r = r[:, :wide]
            keep = (lane2 >= g * HEAD_DIM) & (lane2 < (g + 1) * HEAD_DIM)
            q_s[h] = jnp.where(keep, r, 0.0).astype(jnp.bfloat16)[:, :kw]
        copies[1].wait()
        x = lax.dot_general(wk_ref[...], normed, NT, preferred_element_type=jnp.float32)
        turned = []
        for g in range(kv_heads):
            a = x[g * HEAD_DIM : g * HEAD_DIM + h2]
            b = x[g * HEAD_DIM + h2 : (g + 1) * HEAD_DIM]
            turned += [a * cos_t - b * sin_t, b * cos_t + a * sin_t]
        fresh_k = jnp.concatenate(turned, axis=0).astype(jnp.bfloat16)
        copies[2].wait()
        fresh_v = lax.dot_general(
            wv_ref[...], normed, NT, preferred_element_type=jnp.float32
        ).astype(jnp.bfloat16)
        for part in range(2):
            start = pl.multiple_of((tok if part == 0 else 1 - tok) * half, half)
            nk_ref[:, pl.ds(start, half)] = fresh_k[:, part * half : (part + 1) * half]
            nv_ref[:, pl.ds(start, half)] = fresh_v[:, part * half : (part + 1) * half]

        def token_of(index):
            return index + jnp.where(index < half, tok * half, -tok * half)

        def with_ones(vals):
            return jnp.concatenate(
                [vals, jnp.ones((wide - kw, vals.shape[1]), jnp.bfloat16)], axis=0
            )

        row_t = token_of(lax.broadcasted_iota(jnp.int32, (rows, rows), 0))
        col_t = token_of(lax.broadcasted_iota(jnp.int32, (rows, rows), 1))
        seen = col_t <= row_t
        vals = with_ones(fresh_v)
        for h in range(heads):
            s = jnp.dot(q_s[h], fresh_k, preferred_element_type=jnp.float32) * scale
            s = jnp.where(seen, s, -jnp.inf)
            m = jnp.broadcast_to(jnp.max(s, axis=1, keepdims=True), (rows, 128))
            p = jnp.exp2(s - jnp.concatenate([m] * (rows // 128), axis=1))
            top[h] = m
            acc[h] = lax.dot_general(
                p.astype(jnp.bfloat16), vals, NT, preferred_element_type=jnp.float32
            )

        def block(index, masked):
            start = pl.multiple_of(index * KEY_BLOCK, KEY_BLOCK)
            keys = k_ref[:, pl.ds(start, KEY_BLOCK)]
            vals = with_ones(v_ref[:, pl.ds(start, KEY_BLOCK)])
            if masked:
                row_t = token_of(lax.broadcasted_iota(jnp.int32, (rows, KEY_BLOCK), 0))
                col = start + lax.broadcasted_iota(jnp.int32, (rows, KEY_BLOCK), 1)
                seen = (col > row_t) & (col >= window - length)
            for h in range(heads):
                s = jnp.dot(q_s[h], keys, preferred_element_type=jnp.float32) * scale
                if masked:
                    s = jnp.where(seen, s, -jnp.inf)
                old = top[h]
                m = jnp.maximum(old, jnp.max(s, axis=1, keepdims=True))
                p = jnp.exp2(s - jnp.concatenate([m] * (KEY_BLOCK // 128), axis=1))
                alpha = jnp.exp2(old - m)
                top[h] = m
                acc[h] = acc[h] * jnp.concatenate(
                    [alpha] * (wide // 128), axis=1
                ) + lax.dot_general(
                    p.astype(jnp.bfloat16), vals, NT, preferred_element_type=jnp.float32
                )

        blocks = window // KEY_BLOCK
        first_block = jnp.maximum(window - length, 0) // KEY_BLOCK
        copies[3].wait()
        copies[4].wait()

        @pl.when(first_block < blocks)
        def _():
            block(first_block, True)

        @pl.loop(first_block + 1, blocks)
        def _(index):
            block(index, False)

        total = jnp.zeros((rows, qw), jnp.float32)
        for h in range(heads):
            g = h // group
            a = acc[h]
            o = a / a[:, kw : kw + 1]
            keep = (lane2 >= g * HEAD_DIM) & (lane2 < (g + 1) * HEAD_DIM)
            o = jnp.where(keep, o, 0.0)
            o = jnp.concatenate([o, jnp.zeros((rows, qw - wide), jnp.float32)], axis=1)
            shift = (h * HEAD_DIM - g * HEAD_DIM) % qw
            total = total + (o if shift == 0 else pltpu.roll(o, shift, 1))
        att_ref[...] = total.astype(jnp.bfloat16)


def whole(a):
    return pl.BlockSpec(a.shape, lambda *_: (0,) * a.ndim)


def of_slot(slot, a):
    return pl.BlockSpec((None,) + a.shape[1:], lambda *_: (slot,) + (0,) * (a.ndim - 1))


ANY = pl.BlockSpec(memory_space=pl.ANY)


def attention(slot, scal, hidden, other, gain, cos, sin, wq, wk_t, wv_t, keys_t, values_t):
    half, width = other.shape
    rows = 2 * half
    qw, kw = wq.shape[1], wk_t.shape[0]
    heads, kv_heads = qw // HEAD_DIM, kw // HEAD_DIM
    window = keys_t.shape[2]
    wide = -(-(kw + 1) // 128) * 128
    shapes = [(rows, qw), (kw, rows), (kw, rows)]
    bf16 = jnp.bfloat16
    return pl.pallas_call(
        functools.partial(attention_kernel, kv_heads, heads // kv_heads, slot),
        grid_spec=pltpu.PrefetchScalarGridSpec(
            num_scalar_prefetch=1,
            grid=(1,),
            in_specs=[
                of_slot(slot, hidden),
                whole(other),
                whole(gain),
                of_slot(slot, cos),
                of_slot(slot, sin),
            ]
            + [ANY] * 5,
            out_specs=[pl.BlockSpec(s, lambda *_: (0, 0)) for s in shapes],
            scratch_shapes=[
                pltpu.VMEM((rows, width), bf16),
                pltpu.VMEM((heads, rows, kw), bf16),
                pltpu.VMEM(wq.shape, bf16),
                pltpu.VMEM(wk_t.shape, bf16),
                pltpu.VMEM(wv_t.shape, bf16),
                pltpu.VMEM((kw, window), bf16),
                pltpu.VMEM((kw, window), bf16),
                pltpu.VMEM((heads, rows, wide), jnp.float32),
                pltpu.VMEM((heads, rows, 128), jnp.float32),
                pltpu.SemaphoreType.DMA((5,)),
            ],
        ),
        out_shape=[jax.ShapeDtypeStruct(s, bf16) for s in shapes],
        compiler_params=pltpu.CompilerParams(vmem_limit_bytes=58 * 1024 * 1024),
        cost_estimate=pl.CostEstimate(
            flops=20 * 10**9, bytes_accessed=10 * 10**6, transcendentals=9 * 10**6
        ),
        name="attention",
    )(scal, hidden, other, gain, cos, sin, wq, wk_t, wv_t, keys_t, values_t)


def project_kernel(
    a_ref,
    b_ref,
    own_ref,
    other_ref,
    gain_ref,
    wo_hbm,
    wt_hbm,
    res,
    nrm,
    w_s,
    sems,
):
    half, width = own_ref.shape
    copies = [
        pltpu.make_async_copy(src, w_s.at[i], sems.at[i])
        for i, src in enumerate((wo_hbm, wt_hbm))
    ]
    for copy in copies:
        copy.start()
    for copy in copies:
        copy.wait()
    a = a_ref[...]
    b = jnp.concatenate([b_ref[half:, :], b_ref[:half, :]], axis=0)
    square = jnp.zeros((2 * half, 1), jnp.float32)
    for c in range(0, width, ROW_CHUNK):
        cols = slice(c, c + ROW_CHUNK)
        r = jnp.dot(a, w_s[0, :, cols], preferred_element_type=jnp.float32)
        r = r + jnp.dot(b, w_s[1, :, cols], preferred_element_type=jnp.float32)
        hid = jnp.concatenate([own_ref[:, cols], other_ref[:, cols]], axis=0)
        r = (r + hid.astype(jnp.float32)).astype(jnp.bfloat16)
        res[:, cols] = r
        r = r.astype(jnp.float32)
        square = square + jnp.sum(r * r, axis=1, keepdims=True)
    inv = lax.rsqrt(square / width + EPSILON)
    for c in range(0, width, ROW_CHUNK):
        cols = slice(c, c + ROW_CHUNK)
        r = res[:, cols].astype(jnp.float32)
        nrm[:, cols] = (r * inv * gain_ref[:, cols]).astype(jnp.bfloat16)


def project(slot, a, b, hidden, other, gain, w_out, w_other):
    half, width = other.shape
    shape = (2 * half, width)
    return pl.pallas_call(
        project_kernel,
        grid_spec=pltpu.PrefetchScalarGridSpec(
            num_scalar_prefetch=0,
            grid=(1,),
            in_specs=[whole(a), whole(b), of_slot(slot, hidden), whole(other), whole(gain)]
            + [ANY] * 2,
            out_specs=[pl.BlockSpec(shape, lambda *_: (0, 0))] * 2,
            scratch_shapes=[
                pltpu.VMEM((2,) + w_out.shape, jnp.bfloat16),
                pltpu.SemaphoreType.DMA((2,)),
            ],
        ),
        out_shape=[jax.ShapeDtypeStruct(shape, jnp.bfloat16)] * 2,
        compiler_params=pltpu.CompilerParams(vmem_limit_bytes=32 * 1024 * 1024),
        cost_estimate=pl.CostEstimate(
            flops=4 * 10**9, bytes_accessed=10 * 10**6, transcendentals=10**3
        ),
        name="project",
    )(a, b, hidden, other, gain, w_out, w_other)


def local(
    hidden_in,
    cache_keys,
    stored_cache_values,
    cache_lengths,
    live_slots,
    attn_gain,
    w_query,
    key_weight,
    value_weight,
    w_out,
    mlp_gain,
    w_gate,
    w_up,
    w_down,
):
    slots, half, width = hidden_in.shape
    rows = 2 * half
    tok = lax.axis_index("tok").astype(jnp.int32)
    req = lax.axis_index("req").astype(jnp.int32)
    reqs = lax.axis_size("req")
    swap = [(0, 1), (1, 0)]
    other_half = lambda a: lax.ppermute(a, "tok", swap)

    others = [other_half(hidden_in[0])]
    for s in range(1, slots):
        rest, others[-1] = lax.optimization_barrier((hidden_in[s], others[-1]))
        others.append(other_half(rest))
    share = w_out.shape[0] // reqs
    piece = other_half(lax.dynamic_slice_in_dim(w_out, req * share, share, 0))
    w_other = lax.all_gather(piece, "req", axis=0, tiled=True)

    alive = lax.dynamic_slice_in_dim(live_slots, req * slots, slots)
    index = jnp.arange(rows, dtype=jnp.int32)
    token = index + jnp.where(index < half, tok * half, -tok * half)
    positions = cache_lengths[:, None] + token[None, :]
    h2 = HEAD_DIM // 2
    inverse = ROPE_BASE ** (-(jnp.arange(h2, dtype=jnp.float32) * 2.0) / HEAD_DIM)
    angles = positions.astype(jnp.float32)[:, None, :] * inverse[None, :, None]
    cos, sin = jnp.cos(angles), jnp.sin(angles)

    flip = lambda a: jnp.swapaxes(a, -1, -2)
    keys_t, values_t = flip(cache_keys), flip(stored_cache_values)
    wk_t, wv_t = flip(key_weight), flip(value_weight)
    attended = []
    new_keys = []
    new_values = []
    for s in range(slots):
        scal = jnp.stack([cache_lengths[s], alive[s], tok])
        a, k, v = attention(
            s,
            scal,
            hidden_in,
            others[s],
            attn_gain[None, :],
            cos,
            sin,
            w_query,
            wk_t,
            wv_t,
            keys_t,
            values_t,
        )
        attended.append(a)
        new_keys.append(k)
        new_values.append(v)
    received = [other_half(a) for a in attended]
    results = []
    for s in range(slots):
        residual, mlp_in = project(
            s,
            attended[s],
            received[s],
            hidden_in,
            others[s],
            mlp_gain[None, :],
            w_out,
            w_other,
        )
        gate = jnp.dot(mlp_in, w_gate, preferred_element_type=jnp.float32)
        up = jnp.dot(mlp_in, w_up, preferred_element_type=jnp.float32)
        act = (jax.nn.silu(gate) * up).astype(jnp.bfloat16)
        theirs = jnp.dot(act[half:], w_down, preferred_element_type=jnp.float32)
        theirs = other_half(theirs.astype(jnp.bfloat16))
        mine = jnp.dot(act[:half], w_down, preferred_element_type=jnp.float32)
        out = residual[:half].astype(jnp.float32) + mine + theirs.astype(jnp.float32)
        results.append(jnp.where(alive[s] > 0, out, 0.0).astype(jnp.bfloat16))
    return (jnp.stack(results), flip(jnp.stack(new_keys)), flip(jnp.stack(new_values)))


def solution(mesh):
    return jax.shard_map(
        local,
        mesh=mesh,
        in_specs=(
            P("req", "tok", None),
            P("req", None, "tok"),
            P("req", None, "tok"),
            P("req"),
            P(),
            P(),
            P(None, "tok"),
            P(None, "tok"),
            P(None, "tok"),
            P("tok", None),
            P(),
            P(None, "tok"),
            P(None, "tok"),
            P("tok", None),
        ),
        out_specs=(P("req", "tok", None), P("req", None, "tok"), P("req", None, "tok")),
        check_vma=False,
    )
```
